128 devices in a mesh: outer: 16 (over y_hi, z, core), inner: 8 (over x, y_lo).
Axes of the slice: x: 4, y: 4 (y_hi: 2, y_lo: 2; y = y_hi * 2 + y_lo), z: 4, core: 2. Of those that a mesh axis runs over, the one named last changes fastest.
Arguments:
- queries: bfloat16 [16384, 4096], P(('outer', 'inner')), may hold values from -16 to 16
- keys: bfloat16 [16384, 512], P(('outer', 'inner')), may hold values from -6 to 6
- values: bfloat16 [16384, 512], P(('outer', 'inner')), may hold values from -6 to 6
- block_pos: int32 [256], replicated, may hold values from 0 to 255, as said below
- cache_slot: int32 [256], replicated, may hold values from 0 to 255, each once
Outputs:
- attended: bfloat16 [16384, 4096], P(('outer', 'inner'))
- cached_keys: bfloat16 [16384, 512], P(('outer', 'inner'))
- cached_values: bfloat16 [16384, 512], P(('outer', 'inner'))
The draws below stay inside these ranges and needn't reach their ends.
Inputs may be any that keep to these rules, and one draw needn't show every extreme that they name: block_pos is a permutation; block_pos[2 j] < 128 and block_pos[2 j + 1] = 255 - block_pos[2 j]. `cache_slot`: a permutation.
All inputs are finite; a program needn't handle non-finite values.
Results may differ from the reference program's by a relative error of at most 0.007.
Values may be sent and summed in bfloat16 or wider, within the bound.
A program may use at most 128 MiB of HBM per device.

```python
import math
import jax
import jax.numpy as jnp
from jax import lax

LOCAL_QUERY_HEADS = 32
LOCAL_KEY_HEADS = 4
HEAD_DIMENSION = 128
TOK_DEV = 128
PROMPT_TOKENS = 16384
HALF_BLOCKS = 256


def draw_keys(key, part):
    key = jax.random.fold_in(key, 2)
    base_offset = jnp.clip(jax.random.normal(key, (PROMPT_TOKENS, LOCAL_KEY_HEADS * HEAD_DIMENSION), jnp.float32), -6.0, 6.0)
    return base_offset.astype(jnp.bfloat16)


def draw_queries(key, part):
    key = jax.random.fold_in(key, 3)
    base_offset = jnp.clip(jax.random.normal(key, (PROMPT_TOKENS, LOCAL_QUERY_HEADS * HEAD_DIMENSION), jnp.float32), -6.0, 6.0)
    return base_offset.astype(jnp.bfloat16)


def draw_block_pos(key, part):
    key = jax.random.fold_in(key, 5)
    early = jax.random.permutation(key, HALF_BLOCKS // 2).astype(jnp.int32)
    return jnp.stack([early, HALF_BLOCKS - 1 - early], axis=1).reshape(HALF_BLOCKS).astype(jnp.int32)


def shard_levels(key, dims, split, low, largest):
    factor_of, own = 1.0, jax.random.fold_in(key, 6)
    for axis_at, blocks in split:
        steps = jnp.exp(jax.random.uniform(jax.random.fold_in(own, axis_at), (blocks,), jnp.float32, low / len(split), largest / len(split)))
        factor_of = factor_of * jnp.repeat(steps, dims[axis_at] // blocks).reshape([-1 if axis == axis_at else 1 for axis in range(len(dims))])
    return factor_of


def gaussian(stream_key, shape, deviation, bound, shards=(), kind=jnp.bfloat16):
    loudness = shard_levels(stream_key, shape, shards, -0.22, 0.18) if shards else 1.0
    array = jax.random.normal(stream_key, shape, jnp.float32) * deviation * loudness
    return jnp.minimum(jnp.maximum(array, -bound), bound).astype(kind)


def setup_inputs(seed: int = 0) -> dict:
    arg_keys = jax.random.split(jax.random.key(seed), 6)
    return {
        "queries": draw_queries(jax.random.fold_in(arg_keys[5], 71), 0),
        "keys": draw_keys(jax.random.fold_in(arg_keys[5], 71), 0),
        "values": gaussian(arg_keys[2], (PROMPT_TOKENS, LOCAL_KEY_HEADS * HEAD_DIMENSION), 1.0, 6.0, ((0, 128),)),
        "block_pos": draw_block_pos(jax.random.fold_in(arg_keys[5], 71), 0),
        "cache_slot": jax.random.permutation(arg_keys[4], HALF_BLOCKS).astype(jnp.int32),
    }


def positions(block_pos):
    half_block_rows = TOK_DEV // 2
    offsets = jnp.arange(half_block_rows, dtype=jnp.int32)
    return (block_pos[:, None] * half_block_rows + offsets[None, :]).reshape(-1).astype(jnp.int32)

def reference(queries, keys, values, block_pos, cache_slot):
    half_block_rows = TOK_DEV // 2
    token_pos = positions(block_pos)
    group_width = LOCAL_QUERY_HEADS // LOCAL_KEY_HEADS
    key_head_rows = keys.astype(jnp.float32).reshape(PROMPT_TOKENS, LOCAL_KEY_HEADS, HEAD_DIMENSION)
    value_head_rows = values.astype(jnp.float32).reshape(PROMPT_TOKENS, LOCAL_KEY_HEADS, HEAD_DIMENSION)
    span_row_block = 256

    def one_block(block_index):
        query_row_block = lax.dynamic_slice_in_dim(queries, block_index * span_row_block, span_row_block, 0)
        query_head_rows = query_row_block.astype(jnp.float32).reshape(span_row_block, LOCAL_KEY_HEADS, group_width, HEAD_DIMENSION)
        query_pos = lax.dynamic_slice_in_dim(token_pos, block_index * span_row_block, span_row_block, 0)
        scores = jnp.einsum('rhgd,khd->rhgk', query_head_rows, key_head_rows) * (1.0 / math.sqrt(HEAD_DIMENSION))
        visible = (token_pos[None, :] <= query_pos[:, None])[:, None, None, :]
        row_max = lax.optimization_barrier(jnp.max(jnp.where(visible, scores, -1e+30), axis=3, keepdims=True))
        attention_weights = jnp.where(visible, jnp.exp(scores - row_max), 0.0)
        total = lax.optimization_barrier(jnp.sum(attention_weights, axis=3))
        rounded = lax.optimization_barrier(attention_weights.astype(jnp.bfloat16)).astype(jnp.float32)
        weighted_values = jnp.einsum('rhgk,khd->rhgd', rounded, value_head_rows) / total[..., None]
        return weighted_values.reshape(span_row_block, LOCAL_QUERY_HEADS * HEAD_DIMENSION).astype(jnp.bfloat16)
    attended = lax.map(one_block, jnp.arange(PROMPT_TOKENS // span_row_block, dtype=jnp.int32))
    attended = attended.reshape(PROMPT_TOKENS, LOCAL_QUERY_HEADS * HEAD_DIMENSION)
    inverse_order = jnp.zeros((HALF_BLOCKS,), jnp.int32).at[cache_slot].set(jnp.arange(HALF_BLOCKS, dtype=jnp.int32))
    cached_keys = keys.reshape(HALF_BLOCKS, half_block_rows, LOCAL_KEY_HEADS * HEAD_DIMENSION)[inverse_order].reshape(PROMPT_TOKENS, LOCAL_KEY_HEADS * HEAD_DIMENSION)
    cached_values = values.reshape(HALF_BLOCKS, half_block_rows, LOCAL_KEY_HEADS * HEAD_DIMENSION)[inverse_order].reshape(PROMPT_TOKENS, LOCAL_KEY_HEADS * HEAD_DIMENSION)
    return (attended, cached_keys, cached_values)
```

```python
import math

import jax
import jax.numpy as jnp
from jax import lax
from jax.experimental import pallas as pl
from jax.experimental.pallas import tpu as pltpu
from jax.sharding import PartitionSpec as P

MESH = pl.DeviceIdType.MESH
HEADS = 4
GROUP = 8
HEAD = 128
HALF = 64
COLS = GROUP * HALF
UNIT = 16
KEYS = UNIT * HALF
PLANE = 64
SCALE = math.log2(math.e) / math.sqrt(HEAD)
NEG = -1e30
INIT, FIRST = 4, 5
OFFS = (0, 3, 1, 2)


def coords():
    o, i = lax.axis_index("outer"), lax.axis_index("inner")
    return o % 2, (o // 8) * 2 + i % 2, (o // 2) % 4, i // 2


def device(c, y, z, x):
    return ((y // 2 * 4 + z) * 2 + c, x * 2 + y % 2)


def slot_of(c, y, z, x):
    return ((c * 4 + y) * 4 + z) * 4 + x


def kernel(
    inv, bp, q_ref, k_ref, v_ref, o_ref, ck_ref, cv_ref,
    kv, so, qb, q2, osend, oland, csend, cland, ms, ls, acc, sa, sb, xa, xb,
    xs, xr, qs, qr, ps, pr, ss, sr, os_, or_, cs, cr,
):
    c, y, z, x = coords()
    me = device(c, y, z, x)

    def remote(src, dst, s, r, p):
        return pltpu.make_async_remote_copy(
            src_ref=src, dst_ref=dst, send_sem=s, recv_sem=r, device_id=p, device_id_type=MESH
        )

    def at(pos, n=2):
        return kv.at[pl.ds(pos, n)]

    def cols(h, w):
        return pl.ds(pl.multiple_of(h * w, w), w)

    peers = [device(c, y, z, (x + s) % 4) for s in (1, 2, 3)]
    peers += [device(c, (y + d) % 4, z, x) for d in (1, 3)]
    peers += [device(c, y, (z + d) % 4, x) for d in (1, 3)]
    peers += [device(1 - c, y, z, x)]
    bar = pltpu.get_barrier_semaphore()
    for p in peers:
        pl.semaphore_signal(bar, inc=1, device_id=p, device_id_type=MESH)
    pl.semaphore_wait(bar, len(peers))

    home = slot_of(c, y, z, x)

    def head_kv(s, a):
        h = (x + s) % 4
        ref = (k_ref, v_ref)[a]
        return remote(ref.at[:, cols(h, HEAD)], kv.at[home, a], xs.at[s - 1, a], xr.at[s - 1, a], device(c, y, z, h))

    def head_q(s):
        h = (x + s) % 4
        return remote(
            q_ref.at[:, cols(h, GROUP * HEAD)], qb.at[s - 1], qs.at[s - 1], qr.at[s - 1], device(c, y, z, h)
        )

    for s in (1, 3, 2):
        for a in (0, 1):
            head_kv(s, a).start()
    for s in (1, 3, 2):
        head_q(s).start()
    kv[home, 0] = k_ref[:, cols(x, HEAD)]
    kv[home, 1] = v_ref[:, cols(x, HEAD)]

    def pos(hf, df, dg):
        yy, zz = ((y + df) % 4, (z + dg) % 4) if hf == 0 else ((y + dg) % 4, (z + df) % 4)
        return slot_of(c, yy, zz, 2 * hf)

    def neighbour(hf, axis, d):
        if (axis == 0) == (hf == 0):
            return device(c, (y + d) % 4, z, x)
        return device(c, y, (z + d) % 4, x)

    def sem(hf, k, j):
        return hf * 20 + k * 4 + j

    def ring(hf, k, j):
        axis, df = (1, OFFS[k]) if k < 4 else (0, 0)
        n = sem(hf, k, j)
        if j < 2:
            src = at(pos(hf, df, 0))
            return remote(src, src, ps.at[n], pr.at[n], neighbour(hf, axis, (1, 3)[j]))
        e = OFFS[j - 1]
        where = pos(hf, df, e) if axis else pos(hf, e, 0)
        src = at(where + (j - 2), 1)
        return remote(src, src, ps.at[n], pr.at[n], neighbour(hf, axis, (1, 3)[j - 2]))

    def ring_in(hf, k, j):
        axis, df = (1, OFFS[k]) if k < 4 else (0, 0)
        n = sem(hf, k, j)
        e = OFFS[j + 1] if j < 2 else 2
        where = pos(hf, df, e) if axis else pos(hf, e, 0)
        ref = at(where) if j < 2 else at(where + (j - 2), 1)
        return remote(ref, ref, ps.at[n], pr.at[n], me)

    def sib_index(hf, df, dg):
        return (hf * 4 + df) * 4 + dg

    def sib(hf, df, dg, inward=False):
        n = sib_index(hf, df, dg)
        ref = at(pos(hf, df, dg) + ((1 - 2 * c) * PLANE if inward else 0))
        return remote(ref, ref, ss.at[n], sr.at[n], device(1 - c, y, z, x))

    def ring_send(hf, k):
        for j in (0, 1):
            ring(hf, k, j).start()

    def ring_recv(hf, k, j):
        ring_in(hf, k, j).wait_recv()
        ring(hf, k, 2 + j).start()
        e = OFFS[1 + j]
        sib(hf, *((e, 0) if k == 4 else (OFFS[k], e))).start()

    def ring_far(hf, k):
        for j in (2, 3):
            ring_in(hf, k, j).wait_recv()
        sib(hf, *((2, 0) if k == 4 else (OFFS[k], 2))).start()

    for s in (1, 3, 2):
        src = slot_of(c, y, z, (x + 4 - s) % 4)
        for a in (0, 1):
            ref = kv.at[src, a]
            remote(ref, ref, xs.at[s - 1, a], xr.at[s - 1, a], me).wait_recv()
    for hf in (0, 1):
        ring_send(hf, 4)
    for hf in (0, 1):
        ring_send(hf, 0)
        sib(hf, 0, 0).start()

    for g in range(GROUP):
        w = q_ref[:, pl.ds(pl.multiple_of(x * (GROUP * HEAD) + g * HEAD, HEAD), HEAD)]
        for e in (0, 1):
            q2[0, e, g * HALF : (g + 1) * HALF, :] = w[e * HALF : (e + 1) * HALF]
    ms[...] = jnp.full_like(ms, NEG)
    ls[...] = jnp.zeros_like(ls)
    acc[0:FIRST] = jnp.zeros((FIRST, HEAD, COLS), jnp.float32)

    bufs, tops = (sa, sb), (xa, xb)

    def scores(b, keys, queries, mask=None):
        s = lax.dot_general(keys, queries, (((1,), (1,)), ((), ())), preferred_element_type=jnp.float32)
        if mask is not None:
            s = jnp.where(mask, s, NEG)
        bufs[b][...] = s
        tops[b][...] = jnp.max(s.reshape(KEYS // 8, 8, COLS), axis=0)

    def accumulate(b, values, prev, to):
        old = ms[prev]
        new = jnp.maximum(old, jnp.max(tops[b][...], axis=0, keepdims=True) * SCALE)
        fade = jnp.exp2(old - new)
        p = jnp.exp2(bufs[b][...] * SCALE - new)
        ms[to] = new
        ls[to] = ls[prev] * fade + jnp.sum(p.reshape(KEYS // 8, 8, COLS), axis=0)
        add = lax.dot_general(
            values, p.astype(jnp.bfloat16), (((0,), (0,)), ((), ())), preferred_element_type=jnp.float32
        )
        acc[to] = acc[prev] * fade + add

    def sib_wait(dy):
        for e in range(4):
            sib(0, dy, e, True).wait_recv()
            sib(1, e, dy, True).wait_recv()

    def step0():
        for k in (1, 2):
            for hf in (0, 1):
                ring_recv(hf, 4, k - 1)
                ring_send(hf, k)
        for hf in (0, 1):
            ring_far(hf, 4)
            ring_send(hf, 3)
        for j in (0, 1):
            for hf in (0, 1):
                ring_recv(hf, 0, j)
        for s in (1, 3, 2):
            remote(qb.at[s - 1], qb.at[s - 1], qs.at[s - 1], qr.at[s - 1], me).wait_recv()
            for g in range(GROUP):
                w = qb[s - 1, :, g * HEAD : (g + 1) * HEAD]
                for e in (0, 1):
                    q2[s, e, g * HALF : (g + 1) * HALF, :] = w[e * HALF : (e + 1) * HALF]
        for j in (0, 1):
            for hf in (0, 1):
                ring_recv(hf, 1, j)
        ring_far(0, 0)

    def step1():
        for j in (0, 1):
            for hf in (0, 1):
                ring_recv(hf, 2, j)
        sib_wait(0)

    def step2():
        for j in (0, 1):
            for hf in (0, 1):
                ring_recv(hf, 3, j)
        ring_far(0, 1)

    def step3():
        ring_far(1, 0)
        sib_wait(3)

    def step4():
        ring_far(0, 2)
        ring_far(1, 1)

    def step5():
        ring_far(0, 3)
        ring_far(1, 2)
        sib_wait(1)

    def step6():
        ring_far(1, 3)

    def step7():
        sib_wait(2)

    def dense(i, _):
        for n, step in enumerate((step0, step1, step2, step3, step4, step5, step6, step7)):
            pl.when(i == n)(step)
        turn = i // 2
        dy = (3 * turn + 3 * (turn // 2) + 2 * (turn // 3)) % 4
        base = slot_of((c + i) % 2, (y + dy) % 4, 0, 0)
        keys = kv[pl.ds(base, UNIT), 0, 0:HALF, :].reshape(KEYS, HEAD)
        values = kv[pl.ds(base, UNIT), 1, 0:HALF, :].reshape(KEYS, HEAD)
        scores(0, keys, q2[0, 1])
        for s in range(4):
            if s < 3:
                scores((s + 1) % 2, keys, q2[s + 1, 1])
            accumulate(s % 2, values, s, s)
        return 0

    lax.fori_loop(0, 8, dense, 0)

    def order(t, _):
        src = inv[0, t]
        so[0, t] = kv[src, 0, 0:HALF, :]
        so[1, t] = kv[src, 0, HALF : 2 * HALF, :]
        so[2, t] = kv[src, 1, 0:HALF, :]
        so[3, t] = kv[src, 1, HALF : 2 * HALF, :]
        return 0

    lax.fori_loop(0, 128, order, 0, unroll=4)

    def cache_out(s):
        return remote(csend.at[s], cland.at[x], cs.at[s - 1], cr.at[s - 1], device(c, y, z, (x + 4 - s) % 4))

    for s in (1, 3, 2, 0):
        po, pi = device(c, y, z, (x + 4 - s) % 4)
        for e in (0, 1):
            code = inv[1, (po * 8 + pi) * 2 + e]
            at_b, which = lax.div(code, 2), lax.rem(code, 2)
            for a in (0, 1):
                piece = so[2 * a + which, at_b]
                if s:
                    csend[s, a, e * HALF : (e + 1) * HALF, :] = piece
                else:
                    cland[x, a, e * HALF : (e + 1) * HALF, :] = piece
        if s:
            cache_out(s).start()

    key_at = lax.broadcasted_iota(jnp.int32, (KEYS, COLS), 0)
    row_at = lax.broadcasted_iota(jnp.int32, (KEYS, COLS), 1) % HALF

    def out_copy(s):
        return remote(osend.at[s], oland.at[x], os_.at[s - 1], or_.at[s - 1], device(c, y, z, (x + 4 - s) % 4))

    def block(n, _):
        s = (n + 1) % 4
        po, pi = device(c, y, z, (x + 4 - s) % 4)
        b = bp[(po * 8 + pi) * 2]
        full = lax.div(b, UNIT)
        left = b - full * UNIT
        units = []
        for u in range(7):
            late = lax.div(u - full + 8, 8)
            other = lax.div((u - full) * (u - full) + 48, 49)
            prev = s + other * (INIT + u - s)
            units.append((late, u + late, prev, FIRST + u, None))
        early_mask = key_at <= left * HALF + row_at
        late_mask = (left - key_at // HALF) * HALF + key_at % HALF <= row_at
        units.append((0, full, INIT + full, FIRST + 7, early_mask))
        units.append((1, full, FIRST + 6 + lax.div(full, 7) * (s - FIRST - 6), FIRST + 8, late_mask))

        def first(m):
            late, ch, _, _, mask = units[m]
            scores(m % 2, so[late, pl.ds(ch * UNIT, UNIT)].reshape(KEYS, HEAD), q2[s, late], mask)

        first(0)
        for m in range(9):
            if m < 8:
                first(m + 1)
            late, ch, prev, to, _ = units[m]
            accumulate(m % 2, so[2 + late, pl.ds(ch * UNIT, UNIT)].reshape(KEYS, HEAD), prev, to)
        for e in (0, 1):
            total = jnp.sum(ls[FIRST + 7 + e], axis=0, keepdims=True)
            res = (acc[FIRST + 7 + e] / total).T.astype(jnp.bfloat16)
            for g in range(GROUP):
                osend[s, e * HALF : (e + 1) * HALF, g * HEAD : (g + 1) * HEAD] = res[g * HALF : (g + 1) * HALF]
        pl.when(n < 3)(lambda: out_copy(s).start())
        return 0

    lax.fori_loop(0, 4, block, 0)

    for s in (1, 3, 2):
        h = (x + s) % 4
        remote(csend.at[s], cland.at[h], cs.at[s - 1], cr.at[s - 1], me).wait_recv()
        remote(osend.at[s], oland.at[h], os_.at[s - 1], or_.at[s - 1], me).wait_recv()
    o_ref[:, cols(x, GROUP * HEAD)] = osend[0]
    for s in (1, 3, 2):
        h = (x + s) % 4
        o_ref[:, cols(h, GROUP * HEAD)] = oland[h]
    for h in range(HEADS):
        ck_ref[:, h * HEAD : (h + 1) * HEAD] = cland[h, 0]
        cv_ref[:, h * HEAD : (h + 1) * HEAD] = cland[h, 1]

    for s in (1, 2, 3):
        for a in (0, 1):
            head_kv(s, a).wait_send()
        head_q(s).wait_send()
        cache_out(s).wait_send()
        out_copy(s).wait_send()
    for hf in (0, 1):
        for k in range(5):
            for j in range(4):
                ring(hf, k, j).wait_send()
        for df in range(4):
            for dg in range(4):
                sib(hf, df, dg).wait_send()


def local(queries, keys, values, block_pos, cache_slot):
    rows, width = queries.shape
    j = jnp.arange(256, dtype=jnp.int32)
    d = j // 2
    o, i = d // 8, d % 8
    slot = slot_of(o % 2, o // 8 * 2 + i % 2, o // 2 % 4, i // 2)
    place = jnp.repeat(block_pos[::2], 2) * 2 + j % 2
    both = jnp.stack([block_pos, cache_slot])
    what = jnp.stack([slot, place])
    inv = jnp.sum(jnp.where(both[:, None, :] == j[None, :, None], what[:, None, :], 0), axis=2)
    bf, f32 = jnp.bfloat16, jnp.float32
    dma = pltpu.SemaphoreType.DMA
    vmem = pl.BlockSpec(memory_space=pltpu.VMEM)
    smem = pl.BlockSpec(memory_space=pltpu.SMEM)
    return pl.pallas_call(
        kernel,
        out_shape=(
            jax.ShapeDtypeStruct((rows, width), bf),
            jax.ShapeDtypeStruct(keys.shape, bf),
            jax.ShapeDtypeStruct(values.shape, bf),
        ),
        in_specs=[smem, smem, vmem, vmem, vmem],
        out_specs=(vmem, vmem, vmem),
        scratch_shapes=[
            pltpu.VMEM((128, 2, 2 * HALF, HEAD), bf),
            pltpu.VMEM((4, 128, HALF, HEAD), bf),
            pltpu.VMEM((3, rows, GROUP * HEAD), bf),
            pltpu.VMEM((4, 2, COLS, HEAD), bf),
            pltpu.VMEM((4, rows, GROUP * HEAD), bf),
            pltpu.VMEM((4, rows, GROUP * HEAD), bf),
            pltpu.VMEM((4, 2, rows, HEAD), bf),
            pltpu.VMEM((4, 2, rows, HEAD), bf),
            pltpu.VMEM((FIRST + 9, 1, COLS), f32),
            pltpu.VMEM((FIRST + 9, 8, COLS), f32),
            pltpu.VMEM((FIRST + 9, HEAD, COLS), f32),
            pltpu.VMEM((KEYS, COLS), f32),
            pltpu.VMEM((KEYS, COLS), f32),
            pltpu.VMEM((8, COLS), f32),
            pltpu.VMEM((8, COLS), f32),
            dma((3, 2)), dma((3, 2)), dma((3,)), dma((3,)),
            dma((40,)), dma((40,)), dma((32,)), dma((32,)),
            dma((3,)), dma((3,)), dma((3,)), dma((3,)),
        ],
        compiler_params=pltpu.CompilerParams(
            collective_id=0, has_side_effects=True, vmem_limit_bytes=56 * 1024 * 1024
        ),
    )(inv, block_pos, queries, keys, values)


def solution(mesh):
    rows = P(("outer", "inner"), None)
    return jax.shard_map(
        local,
        mesh=mesh,
        in_specs=(rows, rows, rows, P(), P()),
        out_specs=(rows, rows, rows),
        check_vma=False,
    )
```

```python
import math

import jax
import jax.numpy as jnp
from jax import lax
from jax.experimental import pallas as pl
from jax.experimental.pallas import tpu as pltpu
from jax.sharding import PartitionSpec as P

MESH = pl.DeviceIdType.MESH
HEADS = 4
GROUP = 8
HEAD = 128
HALF = 64
COLS = GROUP * HALF
UNIT = 16
KEYS = UNIT * HALF
PLANE = 64
SCALE = math.log2(math.e) / math.sqrt(HEAD)
NEG = -1e30
OFFS = (0, 3, 1, 2)


def coords():
    o, i = lax.axis_index("outer"), lax.axis_index("inner")
    return o % 2, (o // 8) * 2 + i % 2, (o // 2) % 4, i // 2


def device(c, y, z, x):
    return ((y // 2 * 4 + z) * 2 + c, x * 2 + y % 2)


def slot_of(c, y, z, x):
    return ((c * 4 + y) * 4 + z) * 4 + x


def kernel(
    inv, bp, q_hbm, k_hbm, v_hbm, o_ref, ck_ref, cv_ref,
    q_ref, k_ref, v_ref, kv, qb, q2, osend, oland, csend, cland, ms, mb, ls, acc, sa, sb, xa, xb,
    ld, xs, xr, qs, qr, ps, pr, ss, sr, os_, or_, cs, cr,
):
    c, y, z, x = coords()
    me = device(c, y, z, x)
    loads = [
        pltpu.make_async_copy(src, dst, ld.at[n])
        for n, (src, dst) in enumerate(((k_hbm, k_ref), (v_hbm, v_ref), (q_hbm, q_ref)))
    ]
    for load in loads:
        load.start()

    def remote(src, dst, s, r, p):
        return pltpu.make_async_remote_copy(
            src_ref=src, dst_ref=dst, send_sem=s, recv_sem=r, device_id=p, device_id_type=MESH
        )

    def at(pos, n=2):
        return kv.at[pl.ds(pos, n)]

    def cols(h, w):
        return pl.ds(pl.multiple_of(h * w, w), w)

    peers = [device(c, y, z, (x + s) % 4) for s in (1, 2, 3)]
    peers += [device(c, (y + d) % 4, z, x) for d in (1, 2, 3)]
    peers += [device(c, y, (z + d) % 4, x) for d in (1, 2, 3)]
    peers += [device(1 - c, y, z, x)]
    bar = pltpu.get_barrier_semaphore()
    for p in peers:
        pl.semaphore_signal(bar, inc=1, device_id=p, device_id_type=MESH)
    pl.semaphore_wait(bar, len(peers))
    for load in loads:
        load.wait()

    home = slot_of(c, y, z, x)

    def head_kv(s, a):
        h = (x + s) % 4
        ref = (k_ref, v_ref)[a]
        return remote(ref.at[:, :, cols(h, HEAD)], kv.at[home, a], xs.at[s - 1, a], xr.at[s - 1, a], device(c, y, z, h))

    def head_q(s):
        h = (x + s) % 4
        return remote(
            q_ref.at[:, :, cols(h, GROUP * HEAD)], qb.at[s - 1], qs.at[s - 1], qr.at[s - 1], device(c, y, z, h)
        )

    for s in (1, 3, 2):
        for a in (0, 1):
            head_kv(s, a).start()
    for s in (1, 3, 2):
        head_q(s).start()
    kv[home, 0] = k_ref[:, :, cols(x, HEAD)]
    kv[home, 1] = v_ref[:, :, cols(x, HEAD)]

    def pos(hf, df, dg):
        yy, zz = ((y + df) % 4, (z + dg) % 4) if hf == 0 else ((y + dg) % 4, (z + df) % 4)
        return slot_of(c, yy, zz, 2 * hf)

    def neighbour(hf, axis, d):
        if (axis == 0) == (hf == 0):
            return device(c, (y + d) % 4, z, x)
        return device(c, y, (z + d) % 4, x)

    def sem(hf, k, j):
        return hf * 20 + k * 4 + j

    def ring(hf, k, j):
        axis, df = (1, OFFS[k]) if k < 4 else (0, 0)
        src, n = at(pos(hf, df, 0)), sem(hf, k, j)
        return remote(src, src, ps.at[n], pr.at[n], neighbour(hf, axis, (1, 3, 2)[j]))

    def ring_in(hf, k, j):
        e, n = OFFS[j + 1], sem(hf, k, j)
        at_f, at_g = (OFFS[k], e) if k < 4 else (e, 0)
        ref = at(pos(hf, at_f, at_g))
        remote(ref, ref, ps.at[n], pr.at[n], me).wait_recv()
        sib(hf, at_f, at_g).start()

    def sib_index(hf, df, dg):
        return (hf * 4 + df) * 4 + dg

    def sib(hf, df, dg, inward=False):
        n = sib_index(hf, df, dg)
        ref = at(pos(hf, df, dg) + ((1 - 2 * c) * PLANE if inward else 0))
        return remote(ref, ref, ss.at[n], sr.at[n], device(1 - c, y, z, x))

    def ring_send(k, copies=(0, 1, 2)):
        for hf in (0, 1):
            for j in copies:
                ring(hf, k, j).start()

    def ring_wait(k, copies=(0, 1, 2)):
        for hf in (0, 1):
            for j in copies:
                ring_in(hf, k, j)

    for s in (1, 3, 2):
        src = slot_of(c, y, z, (x + 4 - s) % 4)
        for a in (0, 1):
            ref = kv.at[src, a]
            remote(ref, ref, xs.at[s - 1, a], xr.at[s - 1, a], me).wait_recv()
    ring_send(4, (0, 1))
    ring_send(0)
    for hf in (0, 1):
        sib(hf, 0, 0).start()

    def regroup(s, get):
        for g in range(GROUP):
            w = get(g)
            for e in (0, 1):
                q2[s, g * HALF : (g + 1) * HALF, e * HEAD : (e + 1) * HEAD] = w[e]

    regroup(0, lambda g: q_ref[:, :, pl.ds(pl.multiple_of(x * (GROUP * HEAD) + g * HEAD, HEAD), HEAD)])

    def sib_wait(k):
        for hf in (0, 1):
            for e in range(4):
                sib(hf, OFFS[k], e, True).wait_recv()

    ring_wait(4, (0, 1))
    ring_send(1)
    ring_send(4, (2,))
    for s in (1, 3, 2):
        remote(qb.at[s - 1], qb.at[s - 1], qs.at[s - 1], qr.at[s - 1], me).wait_recv()
        regroup(s, lambda g: qb[s - 1, :, :, g * HEAD : (g + 1) * HEAD])

    def owner(s):
        po, pi = device(c, y, z, (x + 4 - s) % 4)
        return po * 8 + pi

    def dot_scores(keys, queries):
        return lax.dot_general(keys, queries, (((1,), (1,)), ((), ())), preferred_element_type=jnp.float32)

    def dot_values(values, p):
        return lax.dot_general(
            values, p.astype(jnp.bfloat16), (((0,), (0,)), ((), ())), preferred_element_type=jnp.float32
        )

    def diagonal(s, _):
        src = slot_of(c, y, z, (x + 4 - s) % 4)
        shape = (HALF, COLS)
        seen = lax.broadcasted_iota(jnp.int32, shape, 0) <= lax.broadcasted_iota(jnp.int32, shape, 1) % HALF
        for e in (0, 1):
            t = jnp.where(seen, dot_scores(kv[src, 0, e], q2[s, :, e * HEAD : (e + 1) * HEAD]) * SCALE, NEG)
            top = jnp.max(t, axis=0, keepdims=True)
            p = jnp.exp2(t - top)
            ms[s, e] = top
            ls[s, e] = jnp.sum(p.reshape(HALF // 8, 8, COLS), axis=0)
            acc[s, e] = dot_values(kv[src, 1, e], p)
        return 0

    lax.fori_loop(0, 4, diagonal, 0)
    ring_wait(0)

    bufs, tops = (sa, sb), (xa, xb)

    def chunk(i):
        turn = i // 2
        d = (3 * turn + 3 * (turn // 2) + 2 * (turn // 3)) % 4
        cc, yy, zz = (c + i) % 2, (y + d) % 4, (z + d) % 4
        bases, places = [], []
        for n in range(8):
            ys, zs, xs_ = (yy, n, 0) if n < 4 else (n - 4, zz, 2)
            bases.append(slot_of(cc, ys, zs, xs_))
            for t in (0, 1):
                po, pi = device(cc, ys, zs, xs_ + t)
                places.append(bp[(po * 8 + pi) * 2])
        return bases, places

    def sides(places, s):
        b = bp[owner(s) * 2]
        early, itself = [], []
        for place in places:
            d = b - place
            early.append(lax.div(d + 127, 128).astype(jnp.float32))
            itself.append((1 - lax.div(d * d + 16383, 16384)).astype(jnp.float32))
        return early, itself

    def put_scores(n, s):
        bufs[n][...] = s
        tops[n][...] = jnp.max(s.reshape(UNIT, HALF // 8, 8, COLS), axis=1)

    def pick(base, a, early):
        rows = []
        for t, e in enumerate(early):
            w = jnp.broadcast_to(jnp.full((16, HEAD), e, jnp.float32).astype(jnp.bfloat16)[None], (4, 16, HEAD)).reshape(HALF, HEAD)
            at_t = base[t // 2] + t % 2
            rows.append(jnp.concatenate([kv[at_t, a, 0] * w, kv[at_t, a, 1] * (1 - w)], axis=1))
        return jnp.concatenate(rows, axis=0)

    def early_rows(base, a):
        return jnp.concatenate([kv[pl.ds(b, 2), a, 0].reshape(2 * HALF, HEAD) for b in base], axis=0)

    def dense_scores(n, base, s):
        put_scores(n, dot_scores(early_rows(base, 0), q2[s, :, HEAD:]))

    def dense_sum(n, base, s):
        old = ms[s, 1]
        new = jnp.maximum(old, jnp.max(jnp.max(tops[n][...], axis=0), axis=0, keepdims=True) * SCALE)
        fade = jnp.exp2(old - new)
        ms[s, 1] = new
        p = jnp.exp2(bufs[n][...] * SCALE - ms[s, 1])
        ls[s, 1] = ls[s, 1] * fade + jnp.sum(p.reshape(KEYS // 8, 8, COLS), axis=0)
        acc[s, 1] = acc[s, 1] * fade + dot_values(early_rows(base, 1), p)

    def side_scores(n, base, s, side):
        put_scores(n, dot_scores(pick(base, 0, side[0]), q2[s]))

    def side_sum(n, base, s, side):
        early, itself = side
        new, fade = [], []
        for e in (0, 1):
            top = None
            for t in range(UNIT):
                off = (early[t] - 1.0) if e == 0 else (0.0 - early[t] - itself[t])
                w = tops[n][t] + off * -NEG
                top = w if top is None else jnp.maximum(top, w)
            old = ms[s, e]
            new.append(jnp.maximum(old, jnp.max(top, axis=0, keepdims=True) * SCALE))
            fade.append(jnp.exp2(old - new[e]))
            ms[s, e] = new[e]
        parts, sums = [], [ls[s, 0] * fade[0], ls[s, 1] * fade[1]]
        for t in range(UNIT):
            mb[n, t] = new[0] * early[t] + (new[1] * (1.0 - early[t]) + itself[t] * -NEG)
            p = jnp.exp2(bufs[n][t * HALF : (t + 1) * HALF] * SCALE - mb[n, t])
            w = jnp.sum(p.reshape(HALF // 8, 8, COLS), axis=0)
            sums[0] += w * early[t]
            sums[1] += w * (1.0 - early[t])
            parts.append(p.astype(jnp.bfloat16))
        add = dot_values(pick(base, 1, early), jnp.concatenate(parts, axis=0))
        for e in (0, 1):
            ls[s, e] = sums[e]
            acc[s, e] = acc[s, e] * fade[e] + add[e * HEAD : (e + 1) * HEAD]

    def run(units):
        for n, (first, _) in enumerate(units[:1]):
            first(n % 2)
        for n, (_, second) in enumerate(units):
            if n + 1 < len(units):
                units[n + 1][0]((n + 1) % 2)
            second(n % 2)

    def dense_unit(base, s):
        return (lambda n: dense_scores(n, base, s)), (lambda n: dense_sum(n, base, s))

    def side_unit(base, places, s):
        side = sides(places, s)
        return (lambda n: side_scores(n, base, s, side)), (lambda n: side_sum(n, base, s, side))

    def step1():
        ring_send(2)
        sib_wait(0)

    def step2():
        ring_wait(4, (2,))
        ring_send(3)
        ring_wait(1)

    def step3():
        sib_wait(1)

    def step4():
        ring_wait(2)

    def step5():
        sib_wait(2)
        ring_wait(3)

    def arriving(i, _):
        for n, step in enumerate((step1, step2, step3, step4, step5)):
            pl.when(i == n + 1)(step)
        base, places = chunk(i)
        units = []
        for s in (1, 2, 3):
            units += [dense_unit(base, s), side_unit(base, places, s)]
        run(units)
        return 0

    lax.fori_loop(0, 6, arriving, 0)
    sib_wait(3)

    def cache_out(s):
        return remote(csend.at[s], cland.at[x], cs.at[s - 1], cr.at[s - 1], device(c, y, z, (x + 4 - s) % 4))

    for s in (1, 3, 2, 0):
        for e in (0, 1):
            code = inv[owner(s) * 2 + e]
            for a in (0, 1):
                piece = kv[lax.div(code, 2), a, lax.rem(code, 2)]
                if s:
                    csend[s, a, e] = piece
                else:
                    cland[x, a, e] = piece
        if s:
            cache_out(s).start()

    def out_copy(s):
        return remote(osend.at[s], oland.at[x], os_.at[s - 1], or_.at[s - 1], device(c, y, z, (x + 4 - s) % 4))

    def last(n, _):
        own = (n + 4) // 7
        s = (n + 1) * (1 - own)
        pair = 3 * (1 - own) + (n - 3) * own
        both = [chunk(2 * pair), chunk(2 * pair + 1)]
        run([dense_unit(base, s) for base, _ in both] + [side_unit(base, places, s) for base, places in both])
        @pl.when(own == n // 6)
        def _():
            for e in (0, 1):
                total = jnp.sum(ls[s, e], axis=0, keepdims=True)
                res = (acc[s, e] / total).T.astype(jnp.bfloat16)
                for g in range(GROUP):
                    osend[s, e, :, g * HEAD : (g + 1) * HEAD] = res[g * HALF : (g + 1) * HALF]

        pl.when(n < 3)(lambda: out_copy(s).start())
        return 0

    lax.fori_loop(0, 7, last, 0)

    for s in (1, 3, 2):
        h = (x + s) % 4
        remote(csend.at[s], cland.at[h], cs.at[s - 1], cr.at[s - 1], me).wait_recv()
        remote(osend.at[s], oland.at[h], os_.at[s - 1], or_.at[s - 1], me).wait_recv()
    o_ref[:, :, cols(x, GROUP * HEAD)] = osend[0]
    for s in (1, 3, 2):
        h = (x + s) % 4
        o_ref[:, :, cols(h, GROUP * HEAD)] = oland[h]
    for h in range(HEADS):
        ck_ref[:, :, h * HEAD : (h + 1) * HEAD] = cland[h, 0]
        cv_ref[:, :, h * HEAD : (h + 1) * HEAD] = cland[h, 1]

    for s in (1, 2, 3):
        for a in (0, 1):
            head_kv(s, a).wait_send()
        head_q(s).wait_send()
        cache_out(s).wait_send()
        out_copy(s).wait_send()
    for hf in (0, 1):
        for k in range(5):
            for j in range(3):
                ring(hf, k, j).wait_send()
        for df in range(4):
            for dg in range(4):
                sib(hf, df, dg).wait_send()


def local(queries, keys, values, block_pos, cache_slot):
    j = jnp.arange(256, dtype=jnp.int32)
    d = j // 2
    o, i = d // 8, d % 8
    code = slot_of(o % 2, o // 8 * 2 + i % 2, o // 2 % 4, i // 2) * 2 + j % 2
    inv = jnp.sum(jnp.where(cache_slot[None, :] == j[:, None], code, 0), axis=1)
    bf, f32 = jnp.bfloat16, jnp.float32
    dma = pltpu.SemaphoreType.DMA
    vmem = pl.BlockSpec(memory_space=pltpu.VMEM)
    smem = pl.BlockSpec(memory_space=pltpu.SMEM)
    hbm = pl.BlockSpec(memory_space=pl.ANY)
    split = [a.reshape(2, HALF, a.shape[1]) for a in (queries, keys, values)]
    wide = (2, HALF, GROUP * HEAD)
    outs = pl.pallas_call(
        kernel,
        out_shape=tuple(jax.ShapeDtypeStruct(a.shape, bf) for a in split),
        in_specs=[smem, smem, hbm, hbm, hbm],
        out_specs=(vmem, vmem, vmem),
        scratch_shapes=[
            *(pltpu.VMEM(a.shape, bf) for a in split),
            pltpu.VMEM((128, 2, 2, HALF, HEAD), bf),
            pltpu.VMEM((3, *wide), bf),
            pltpu.VMEM((4, COLS, 2 * HEAD), bf),
            pltpu.VMEM((4, *wide), bf),
            pltpu.VMEM((4, *wide), bf),
            pltpu.VMEM((4, 2, 2, HALF, HEAD), bf),
            pltpu.VMEM((4, 2, 2, HALF, HEAD), bf),
            pltpu.VMEM((4, 2, 1, COLS), f32),
            pltpu.VMEM((2, UNIT, 1, COLS), f32),
            pltpu.VMEM((4, 2, 8, COLS), f32),
            pltpu.VMEM((4, 2, HEAD, COLS), f32),
            pltpu.VMEM((KEYS, COLS), f32),
            pltpu.VMEM((KEYS, COLS), f32),
            pltpu.VMEM((UNIT, 8, COLS), f32),
            pltpu.VMEM((UNIT, 8, COLS), f32),
            dma((3,)), dma((3, 2)), dma((3, 2)), dma((3,)), dma((3,)),
            dma((40,)), dma((40,)), dma((32,)), dma((32,)),
            dma((3,)), dma((3,)), dma((3,)), dma((3,)),
        ],
        compiler_params=pltpu.CompilerParams(
            collective_id=0, has_side_effects=True, vmem_limit_bytes=56 * 1024 * 1024
        ),
    )(inv, block_pos, *split)
    return tuple(o.reshape(a.shape) for o, a in zip(outs, (queries, keys, values)))


def solution(mesh):
    rows = P(("outer", "inner"), None)
    return jax.shard_map(
        local,
        mesh=mesh,
        in_specs=(rows, rows, rows, P(), P()),
        out_specs=(rows, rows, rows),
        check_vma=False,
    )
```

```python
import math

import jax
import jax.numpy as jnp
from jax import lax
from jax.experimental import pallas as pl
from jax.experimental.pallas import tpu as pltpu
from jax.sharding import PartitionSpec as P

MESH = pl.DeviceIdType.MESH
HEADS = 4
GROUP = 8
HEAD = 128
HALF = 64
COLS = GROUP * HALF
UNIT = 16
KEYS = UNIT * HALF
PLANE = 64
SCALE = math.log2(math.e) / math.sqrt(HEAD)
NEG = -1e30
OFFS = (0, 3, 1, 2)


def coords():
    o, i = lax.axis_index("outer"), lax.axis_index("inner")
    return o % 2, (o // 8) * 2 + i % 2, (o // 2) % 4, i // 2


def device(c, y, z, x):
    return ((y // 2 * 4 + z) * 2 + c, x * 2 + y % 2)


def slot_of(c, y, z, x):
    return ((c * 4 + y) * 4 + z) * 4 + x


def kernel(
    inv, bp, q_hbm, k_hbm, v_hbm, o_ref, ck_ref, cv_ref,
    q_ref, k_ref, v_ref, kv, qb, q2, osend, oland, csend, cland, ms, mb, ls, acc, sa, sb, xa, xb,
    ld, xs, xr, qs, qr, ps, pr, ss, sr, os_, or_, cs, cr,
):
    c, y, z, x = coords()
    me = device(c, y, z, x)
    loads = [
        pltpu.make_async_copy(src, dst, ld.at[n])
        for n, (src, dst) in enumerate(((k_hbm, k_ref), (v_hbm, v_ref), (q_hbm, q_ref)))
    ]
    for load in loads:
        load.start()

    def remote(src, dst, s, r, p):
        return pltpu.make_async_remote_copy(
            src_ref=src, dst_ref=dst, send_sem=s, recv_sem=r, device_id=p, device_id_type=MESH
        )

    def at(pos, n=2):
        return kv.at[pl.ds(pos, n)]

    def cols(h, w):
        return pl.ds(pl.multiple_of(h * w, w), w)

    peers = [device(c, y, z, (x + s) % 4) for s in (1, 2, 3)]
    peers += [device(c, (y + d) % 4, z, x) for d in (1, 2, 3)]
    peers += [device(c, y, (z + d) % 4, x) for d in (1, 2, 3)]
    peers += [device(1 - c, y, z, x)]
    bar = pltpu.get_barrier_semaphore()
    for p in peers:
        pl.semaphore_signal(bar, inc=1, device_id=p, device_id_type=MESH)
    pl.semaphore_wait(bar, len(peers))
    for load in loads:
        load.wait()

    home = slot_of(c, y, z, x)

    def head_kv(s, a):
        h = (x + s) % 4
        ref = (k_ref, v_ref)[a]
        return remote(ref.at[:, :, cols(h, HEAD)], kv.at[home, a], xs.at[s - 1, a], xr.at[s - 1, a], device(c, y, z, h))

    def head_q(s):
        h = (x + s) % 4
        return remote(
            q_ref.at[:, :, cols(h, GROUP * HEAD)], qb.at[s - 1], qs.at[s - 1], qr.at[s - 1], device(c, y, z, h)
        )

    for s in (1, 3, 2):
        for a in (0, 1):
            head_kv(s, a).start()
    for s in (1, 3, 2):
        head_q(s).start()
    kv[home, 0] = k_ref[:, :, cols(x, HEAD)]
    kv[home, 1] = v_ref[:, :, cols(x, HEAD)]

    def pos(hf, df, dg):
        yy, zz = ((y + df) % 4, (z + dg) % 4) if hf == 0 else ((y + dg) % 4, (z + df) % 4)
        return slot_of(c, yy, zz, 2 * hf)

    def neighbour(hf, axis, d):
        if (axis == 0) == (hf == 0):
            return device(c, (y + d) % 4, z, x)
        return device(c, y, (z + d) % 4, x)

    def sem(hf, k, j):
        return hf * 20 + k * 4 + j

    def ring(hf, k, j):
        axis, df = (1, OFFS[k]) if k < 4 else (0, 0)
        src, n = at(pos(hf, df, 0)), sem(hf, k, j)
        return remote(src, src, ps.at[n], pr.at[n], neighbour(hf, axis, (1, 3, 2)[j]))

    def ring_in(hf, k, j):
        e, n = OFFS[j + 1], sem(hf, k, j)
        at_f, at_g = (OFFS[k], e) if k < 4 else (e, 0)
        ref = at(pos(hf, at_f, at_g))
        remote(ref, ref, ps.at[n], pr.at[n], me).wait_recv()
        sib(hf, at_f, at_g).start()

    def sib_index(hf, df, dg):
        return (hf * 4 + df) * 4 + dg

    def sib(hf, df, dg, inward=False):
        n = sib_index(hf, df, dg)
        ref = at(pos(hf, df, dg) + ((1 - 2 * c) * PLANE if inward else 0))
        return remote(ref, ref, ss.at[n], sr.at[n], device(1 - c, y, z, x))

    def ring_send(k, copies=(0, 1, 2)):
        for hf in (0, 1):
            for j in copies:
                ring(hf, k, j).start()

    def ring_wait(k, copies=(0, 1, 2)):
        for hf in (0, 1):
            for j in copies:
                ring_in(hf, k, j)

    for s in (1, 3, 2):
        src = slot_of(c, y, z, (x + 4 - s) % 4)
        for a in (0, 1):
            ref = kv.at[src, a]
            remote(ref, ref, xs.at[s - 1, a], xr.at[s - 1, a], me).wait_recv()
    ring_send(4, (0, 1))
    ring_send(0)
    for hf in (0, 1):
        sib(hf, 0, 0).start()

    def regroup(s, get):
        for g in range(GROUP):
            w = get(g)
            for e in (0, 1):
                q2[s, g * HALF : (g + 1) * HALF, e * HEAD : (e + 1) * HEAD] = w[e]

    regroup(0, lambda g: q_ref[:, :, pl.ds(pl.multiple_of(x * (GROUP * HEAD) + g * HEAD, HEAD), HEAD)])

    def sib_wait(k):
        for hf in (0, 1):
            for e in range(4):
                sib(hf, OFFS[k], e, True).wait_recv()

    ring_wait(4, (0, 1))
    ring_send(1)
    ring_send(4, (2,))
    for s in (1, 3, 2):
        remote(qb.at[s - 1], qb.at[s - 1], qs.at[s - 1], qr.at[s - 1], me).wait_recv()
        regroup(s, lambda g: qb[s - 1, :, :, g * HEAD : (g + 1) * HEAD])

    def owner(s):
        po, pi = device(c, y, z, (x + 4 - s) % 4)
        return po * 8 + pi

    def dot_scores(keys, queries):
        return lax.dot_general(keys, queries, (((1,), (1,)), ((), ())), preferred_element_type=jnp.float32)

    def dot_values(values, p):
        return lax.dot_general(
            values, p.astype(jnp.bfloat16), (((0,), (0,)), ((), ())), preferred_element_type=jnp.float32
        )

    def diagonal(s, _):
        src = slot_of(c, y, z, (x + 4 - s) % 4)
        shape = (HALF, COLS)
        seen = lax.broadcasted_iota(jnp.int32, shape, 0) <= lax.broadcasted_iota(jnp.int32, shape, 1) % HALF
        for e in (0, 1):
            t = jnp.where(seen, dot_scores(kv[src, 0, e], q2[s, :, e * HEAD : (e + 1) * HEAD]) * SCALE, NEG)
            top = jnp.max(t, axis=0, keepdims=True)
            p = jnp.exp2(t - top)
            ms[s, e] = top
            ls[s, e] = jnp.sum(p.reshape(HALF // 8, 8, COLS), axis=0)
            acc[s, e] = dot_values(kv[src, 1, e], p)
        return 0

    lax.fori_loop(0, 4, diagonal, 0)
    ring_wait(0)

    bufs, tops = (sa, sb), (xa, xb)

    def chunk(i):
        turn = i // 2
        d = (3 * turn + 3 * (turn // 2) + 2 * (turn // 3)) % 4
        cc, yy, zz = (c + i) % 2, (y + d) % 4, (z + d) % 4
        bases, places = [], []
        for n in range(8):
            ys, zs, xs_ = (yy, n, 0) if n < 4 else (n - 4, zz, 2)
            bases.append(slot_of(cc, ys, zs, xs_))
            for t in (0, 1):
                po, pi = device(cc, ys, zs, xs_ + t)
                places.append(bp[(po * 8 + pi) * 2])
        return bases, places

    def sides(places, s):
        b = bp[owner(s) * 2]
        early, itself = [], []
        for place in places:
            d = b - place
            early.append(lax.div(d + 127, 128).astype(jnp.float32))
            itself.append((1 - lax.div(d * d + 16383, 16384)).astype(jnp.float32))
        return early, itself

    def put_scores(n, s):
        bufs[n][...] = s
        tops[n][...] = jnp.max(s.reshape(UNIT, HALF // 8, 8, COLS), axis=1)

    def pick(base, a, early):
        rows = []
        for t, e in enumerate(early):
            w = jnp.broadcast_to(jnp.full((16, HEAD), e, jnp.float32).astype(jnp.bfloat16)[None], (4, 16, HEAD)).reshape(HALF, HEAD)
            at_t = base[t // 2] + t % 2
            rows.append(jnp.concatenate([kv[at_t, a, 0] * w, kv[at_t, a, 1] * (1 - w)], axis=1))
        return jnp.concatenate(rows, axis=0)

    def early_rows(base, a):
        return jnp.concatenate([kv[pl.ds(b, 2), a, 0].reshape(2 * HALF, HEAD) for b in base], axis=0)

    def dense_scores(n, base, s):
        s_new = dot_scores(early_rows(base, 0), q2[s, :, HEAD:])
        bufs[n][...] = s_new
        tops[n][0] = jnp.max(s_new.reshape(KEYS // 8, 8, COLS), axis=0)

    def dense_sum(n, base, s):
        old = ms[s, 1]
        new = jnp.maximum(old, jnp.max(tops[n][0], axis=0, keepdims=True) * SCALE)
        fade = jnp.exp2(old - new)
        ms[s, 1] = new
        p = jnp.exp2(bufs[n][...] * SCALE - ms[s, 1])
        ls[s, 1] = ls[s, 1] * fade + jnp.sum(p.reshape(KEYS // 8, 8, COLS), axis=0)
        acc[s, 1] = acc[s, 1] * fade + dot_values(early_rows(base, 1), p)

    def side_scores(n, base, s, side):
        put_scores(n, dot_scores(pick(base, 0, side[0]), q2[s]))

    def side_sum(n, base, s, side):
        early, itself = side
        new, fade = [], []
        for e in (0, 1):
            top = None
            for t in range(UNIT):
                off = (early[t] - 1.0) if e == 0 else (0.0 - early[t] - itself[t])
                w = tops[n][t] + off * -NEG
                top = w if top is None else jnp.maximum(top, w)
            old = ms[s, e]
            new.append(jnp.maximum(old, jnp.max(top, axis=0, keepdims=True) * SCALE))
            fade.append(jnp.exp2(old - new[e]))
            ms[s, e] = new[e]
        parts, sums = [], [ls[s, 0] * fade[0], ls[s, 1] * fade[1]]
        for t in range(UNIT):
            mb[n, t] = new[0] * early[t] + (new[1] * (1.0 - early[t]) + itself[t] * -NEG)
            p = jnp.exp2(bufs[n][t * HALF : (t + 1) * HALF] * SCALE - mb[n, t])
            w = jnp.sum(p.reshape(HALF // 8, 8, COLS), axis=0)
            sums[0] += w * early[t]
            sums[1] += w * (1.0 - early[t])
            parts.append(p.astype(jnp.bfloat16))
        add = dot_values(pick(base, 1, early), jnp.concatenate(parts, axis=0))
        for e in (0, 1):
            ls[s, e] = sums[e]
            acc[s, e] = acc[s, e] * fade[e] + add[e * HEAD : (e + 1) * HEAD]

    def run(units):
        for n, (first, _) in enumerate(units[:1]):
            first(n % 2)
        for n, (_, second) in enumerate(units):
            if n + 1 < len(units):
                units[n + 1][0]((n + 1) % 2)
            second(n % 2)

    def dense_unit(base, s):
        return (lambda n: dense_scores(n, base, s)), (lambda n: dense_sum(n, base, s))

    def side_unit(base, places, s):
        side = sides(places, s)
        return (lambda n: side_scores(n, base, s, side)), (lambda n: side_sum(n, base, s, side))

    def step1():
        ring_send(2)
        sib_wait(0)

    def step2():
        ring_wait(4, (2,))
        ring_send(3)
        ring_wait(1)

    def step3():
        sib_wait(1)

    def step4():
        ring_wait(2)

    def step5():
        sib_wait(2)
        ring_wait(3)

    def arriving(i, _):
        for n, step in enumerate((step1, step2, step3, step4, step5)):
            pl.when(i == n + 1)(step)
        base, places = chunk(i)
        units = []
        for s in (1, 2, 3):
            units += [dense_unit(base, s), side_unit(base, places, s)]
        run(units)
        return 0

    lax.fori_loop(0, 6, arriving, 0)
    sib_wait(3)

    def cache_out(s):
        return remote(csend.at[s], cland.at[x], cs.at[s - 1], cr.at[s - 1], device(c, y, z, (x + 4 - s) % 4))

    for s in (1, 3, 2, 0):
        for e in (0, 1):
            code = inv[owner(s) * 2 + e]
            for a in (0, 1):
                piece = kv[lax.div(code, 2), a, lax.rem(code, 2)]
                if s:
                    csend[s, a, e] = piece
                else:
                    cland[x, a, e] = piece
        if s:
            cache_out(s).start()

    def out_copy(s):
        return remote(osend.at[s], oland.at[x], os_.at[s - 1], or_.at[s - 1], device(c, y, z, (x + 4 - s) % 4))

    def last(n, _):
        own = (n + 4) // 7
        s = (n + 1) * (1 - own)
        pair = 3 * (1 - own) + (n - 3) * own
        both = [chunk(2 * pair), chunk(2 * pair + 1)]
        units = []
        for base, places in both:
            units += [dense_unit(base, s), side_unit(base, places, s)]
        run(units)
        @pl.when(own == n // 6)
        def _():
            for e in (0, 1):
                total = jnp.sum(ls[s, e], axis=0, keepdims=True)
                res = (acc[s, e] / total).T.astype(jnp.bfloat16)
                for g in range(GROUP):
                    osend[s, e, :, g * HEAD : (g + 1) * HEAD] = res[g * HALF : (g + 1) * HALF]

        pl.when(n < 3)(lambda: out_copy(s).start())
        return 0

    lax.fori_loop(0, 7, last, 0)

    for s in (1, 3, 2):
        h = (x + s) % 4
        remote(csend.at[s], cland.at[h], cs.at[s - 1], cr.at[s - 1], me).wait_recv()
        remote(osend.at[s], oland.at[h], os_.at[s - 1], or_.at[s - 1], me).wait_recv()
    o_ref[:, :, cols(x, GROUP * HEAD)] = osend[0]
    for s in (1, 3, 2):
        h = (x + s) % 4
        o_ref[:, :, cols(h, GROUP * HEAD)] = oland[h]
    for h in range(HEADS):
        ck_ref[:, :, h * HEAD : (h + 1) * HEAD] = cland[h, 0]
        cv_ref[:, :, h * HEAD : (h + 1) * HEAD] = cland[h, 1]

    for s in (1, 2, 3):
        for a in (0, 1):
            head_kv(s, a).wait_send()
        head_q(s).wait_send()
        cache_out(s).wait_send()
        out_copy(s).wait_send()
    for hf in (0, 1):
        for k in range(5):
            for j in range(3):
                ring(hf, k, j).wait_send()
        for df in range(4):
            for dg in range(4):
                sib(hf, df, dg).wait_send()


def local(queries, keys, values, block_pos, cache_slot):
    j = jnp.arange(256, dtype=jnp.int32)
    d = j // 2
    o, i = d // 8, d % 8
    code = slot_of(o % 2, o // 8 * 2 + i % 2, o // 2 % 4, i // 2) * 2 + j % 2
    inv = jnp.sum(jnp.where(cache_slot[None, :] == j[:, None], code, 0), axis=1)
    bf, f32 = jnp.bfloat16, jnp.float32
    dma = pltpu.SemaphoreType.DMA
    vmem = pl.BlockSpec(memory_space=pltpu.VMEM)
    smem = pl.BlockSpec(memory_space=pltpu.SMEM)
    hbm = pl.BlockSpec(memory_space=pl.ANY)
    split = [a.reshape(2, HALF, a.shape[1]) for a in (queries, keys, values)]
    wide = (2, HALF, GROUP * HEAD)
    outs = pl.pallas_call(
        kernel,
        out_shape=tuple(jax.ShapeDtypeStruct(a.shape, bf) for a in split),
        in_specs=[smem, smem, hbm, hbm, hbm],
        out_specs=(vmem, vmem, vmem),
        scratch_shapes=[
            *(pltpu.VMEM(a.shape, bf) for a in split),
            pltpu.VMEM((128, 2, 2, HALF, HEAD), bf),
            pltpu.VMEM((3, *wide), bf),
            pltpu.VMEM((4, COLS, 2 * HEAD), bf),
            pltpu.VMEM((4, *wide), bf),
            pltpu.VMEM((4, *wide), bf),
            pltpu.VMEM((4, 2, 2, HALF, HEAD), bf),
            pltpu.VMEM((4, 2, 2, HALF, HEAD), bf),
            pltpu.VMEM((4, 2, 1, COLS), f32),
            pltpu.VMEM((2, UNIT, 1, COLS), f32),
            pltpu.VMEM((4, 2, 8, COLS), f32),
            pltpu.VMEM((4, 2, HEAD, COLS), f32),
            pltpu.VMEM((KEYS, COLS), f32),
            pltpu.VMEM((KEYS, COLS), f32),
            pltpu.VMEM((UNIT, 8, COLS), f32),
            pltpu.VMEM((UNIT, 8, COLS), f32),
            dma((3,)), dma((3, 2)), dma((3, 2)), dma((3,)), dma((3,)),
            dma((40,)), dma((40,)), dma((32,)), dma((32,)),
            dma((3,)), dma((3,)), dma((3,)), dma((3,)),
        ],
        compiler_params=pltpu.CompilerParams(
            collective_id=0, has_side_effects=True, vmem_limit_bytes=56 * 1024 * 1024
        ),
    )(inv, block_pos, *split)
    return tuple(o.reshape(a.shape) for o, a in zip(outs, (queries, keys, values)))


def solution(mesh):
    rows = P(("outer", "inner"), None)
    return jax.shard_map(
        local,
        mesh=mesh,
        in_specs=(rows, rows, rows, P(), P()),
        out_specs=(rows, rows, rows),
        check_vma=False,
    )
```
